128 devices in a mesh: row: 16 (over x, z), col: 8 (over y, core).
Axes of the slice: x: 4, y: 4, z: 4, core: 2. Of those that a mesh axis runs over, the one named last changes fastest.
Arguments:
- kernel: bfloat16 [8, 16, 192, 24576], P(None, 'row', None, 'col'), may hold values from -1 to 4
- right_side: float32 [8, 3072, 512], P('col', 'row'), may hold values from -6 to 6
- initial: float32 [8, 3072, 512], P('col', 'row'), may hold values from -3 to 3
- local_inverse: float32 [128, 384, 384], P(('row', 'col')), may hold values from -1 to 2
- block_lists: int32 [128, 3], P(('row', 'col')), may hold values from 0 to 191, as said below
- counts: int32 [192], replicated, may hold values from 1 to 16, as said below
Outputs:
- solution: float32 [8, 3072, 512], P('col', 'row')
- residual: float32 [8, 3072, 512], P('col', 'row')
The draws below stay inside these ranges and needn't reach their ends.
Inputs may be any that keep to these rules, and one draw needn't show every extreme that they name: `block_lists`: the blocks of one subdomain are different. With d = s // 1 and p = d mod (8), every block of subdomain s lies among blocks p * 24 to (p + 1) * 24 - 1. Every block is named by some subdomain. counts[q] is the number of pairs (s, k) with block_lists[s, k] = q.
All inputs are finite; a program needn't handle non-finite values.
Results may differ from the reference program's by a relative error of at most 0.023.
Values may be sent and summed in bfloat16 or wider, within the bound.
No kernel may reach another device: no remote copies, remote signals or barrier semaphores. Data moves between devices by JAX's collectives and lax.ppermute only.
A program may use at most 128 MiB of HBM per device.

```python
import math
import jax
import jax.numpy as jnp
from jax import lax

ORDER = 24576
RHS = 512
BLOCK = 128
SPAN = 3
SUBDOMAINS = 128
BLOCKS = 192
PANEL_ROWS = 3072
OWN_ROWS = 192
SUB_DEV = 1


def subdomain_blocks(key):
    panels = ORDER // PANEL_ROWS
    per_panel = SUBDOMAINS // panels
    panel_width = PANEL_ROWS // BLOCK
    common = panel_width - 1
    slot_index = jnp.arange(per_panel)

    def one_panel(panel_key, panel_number):
        order_key, offset_key, pick_key = jax.random.split(panel_key, 3)
        shuffled = jax.random.permutation(order_key, panel_width)
        offsets = jax.random.randint(offset_key, (per_panel,), 0, common - 2)
        coins = jax.random.randint(pick_key, (per_panel,), 0, 2)
        first_block = shuffled[2 * slot_index % common]
        second_block = shuffled[(2 * slot_index + 1) % common]
        spread_block = shuffled[(2 * slot_index + 2 + offsets) % common]
        hot_slot = (panel_number == 0) | (slot_index == 0) | (coins == 1)
        third_block = jnp.where(hot_slot, shuffled[common], spread_block)
        return jnp.stack([first_block, second_block, third_block], axis=1) + panel_number * panel_width
    table = jax.vmap(one_panel)(jax.random.split(key, panels), jnp.arange(panels))
    subdomain_index = jnp.arange(SUBDOMAINS)
    device_number = subdomain_index // SUB_DEV
    panel_of = device_number % panels
    within = device_number // panels * SUB_DEV + subdomain_index % SUB_DEV
    return table[panel_of, within].astype(jnp.int32)


def draw_block_lists(key, part):
    return subdomain_blocks(key)


def draw_counts(key, part):
    flat_ids = subdomain_blocks(key).reshape(-1)
    return jnp.sum((flat_ids[:, None] == jnp.arange(BLOCKS)[None, :]).astype(jnp.int32), axis=0).astype(jnp.int32)


def draw_kernel(key, part):
    key = jax.random.fold_in(key, 11)
    noise_key, diagonal_key = jax.random.split(key)
    spread = 0.6 / math.sqrt(ORDER)
    noise = jax.random.normal(noise_key, (ORDER, ORDER), jnp.float32) * spread
    diagonal = jnp.exp(jax.random.uniform(diagonal_key, (ORDER,), jnp.float32, 0.0, math.log(3.0)))
    places = jnp.arange(ORDER)
    matrix = noise + jnp.where(places[:, None] == places[None, :], diagonal[:, None], 0.0)
    return matrix.reshape(ORDER // PANEL_ROWS, PANEL_ROWS // OWN_ROWS, OWN_ROWS, ORDER).astype(jnp.bfloat16)


def draw_local_inverse(key, part):
    key = jax.random.fold_in(key, 23)
    noise_key, diagonal_key = jax.random.split(key)
    size_local = SPAN * BLOCK
    spread = 0.3 / math.sqrt(size_local)
    noise = jax.random.normal(noise_key, (SUBDOMAINS, size_local, size_local), jnp.float32) * spread
    diagonal = jnp.exp(jax.random.uniform(diagonal_key, (SUBDOMAINS, size_local), jnp.float32, math.log(0.4), math.log(1.2)))
    places = jnp.arange(size_local)
    same = places[:, None] == places[None, :]
    return (noise + jnp.where(same[None, :, :], diagonal[:, :, None], 0.0)).astype(jnp.float32)


def shard_levels(own_key, extent, shards, low, high):
    level = 1.0
    for position, blocks in shards:
        draws = jax.random.uniform(jax.random.fold_in(jax.random.fold_in(own_key, 6), position), (blocks,), jnp.float32, low / len(shards), high / len(shards))
        level = level * jnp.repeat(jnp.exp(draws), extent[position] // blocks).reshape((-1,) + (1,) * (len(extent) - 1 - position))
    return level


def centred(key, extent, scale, reach, cuts=(), kind=jnp.bfloat16):
    entries = jax.random.normal(key, extent, jnp.float32) * scale
    if len(cuts) > 0:
        entries = shard_levels(key, extent, cuts, -0.22, 0.18) * entries
    return jnp.clip(entries, min=-reach, max=reach).astype(kind)


def setup_inputs(seed: int = 0) -> dict:
    keys = jax.random.split(jax.random.key(seed), 7)
    kernel = draw_kernel(jax.random.fold_in(keys[6], 71), 0)
    right_side = centred(keys[1], (ORDER // PANEL_ROWS, PANEL_ROWS, RHS), 1.0, 6.0, ((0, 8), (1, 16)), jnp.float32)
    initial = centred(keys[2], (ORDER // PANEL_ROWS, PANEL_ROWS, RHS), 0.5, 3.0, ((0, 8), (1, 16)), jnp.float32)
    local_inverse = draw_local_inverse(jax.random.fold_in(keys[6], 71), 0)
    block_lists = draw_block_lists(jax.random.fold_in(keys[6], 71), 0)
    counts = draw_counts(jax.random.fold_in(keys[6], 71), 0)
    return {"kernel": kernel, "right_side": right_side, "initial": initial, "local_inverse": local_inverse, "block_lists": block_lists, "counts": counts}


def reference(kernel, right_side, initial, local_inverse, block_lists, counts):
    matrix = kernel.reshape(ORDER, ORDER)
    target = right_side.reshape(ORDER, RHS)
    solution = initial.reshape(ORDER, RHS)
    row_counts = jnp.repeat(counts.astype(jnp.float32), BLOCK)[:, None]
    flat_ids = block_lists.reshape(-1).astype(jnp.int32)

    def apply_kernel(current):
        rounded = lax.optimization_barrier(current.astype(jnp.bfloat16)).astype(jnp.float32)

        def row_block(rows):
            return jnp.dot(rows.astype(jnp.float32), rounded, precision=lax.Precision.HIGHEST)

        return lax.map(row_block, matrix.reshape(16, ORDER // 16, ORDER)).reshape(ORDER, RHS)

    def corrections(current_residual):
        rounded = lax.optimization_barrier(current_residual.astype(jnp.bfloat16)).astype(jnp.float32)
        blocks = rounded.reshape(BLOCKS, BLOCK, RHS)
        picked = blocks[flat_ids].reshape(SUBDOMAINS, SPAN * BLOCK, RHS)
        fix_blocks = jnp.einsum("sab,sbc->sac", local_inverse.astype(jnp.float32), picked, precision=lax.Precision.HIGHEST)
        summed = jnp.zeros((BLOCKS, BLOCK * RHS), jnp.float32).at[flat_ids].add(fix_blocks.reshape(SUBDOMAINS * SPAN, BLOCK * RHS))
        return summed.reshape(ORDER, RHS)

    first_residual = target - apply_kernel(solution)
    solution = solution + corrections(first_residual) / row_counts
    residual = target - apply_kernel(solution)
    solution = solution + corrections(residual) / row_counts
    layout = (ORDER // PANEL_ROWS, PANEL_ROWS, RHS)
    return solution.reshape(layout), residual.reshape(layout)
```

```python
import jax
import jax.numpy as jnp
from jax import lax
from jax.experimental import pallas as pl
from jax.experimental.pallas import tpu as pltpu
from jax.sharding import Mesh, PartitionSpec as P

BLOCK = 128
F32 = jnp.float32
BF16 = jnp.bfloat16
ANY = pl.BlockSpec(memory_space=pl.ANY)
VMEM_LIMIT = 40 * 1024 * 1024
SLOT_STEPS = (0, -1, 1, 2)
PANEL_STEPS = (2, 1, 3, 0)


def ring(value, axis, step):
    return lax.ppermute(value, axis, [(i, (i + step) % 4) for i in range(4)])


def cross(value):
    return lax.ppermute(value, "core", [(0, 1), (1, 0)])


def gather_ring(own, first, second, split):
    left, right = ring(own, first, 1), ring(own, first, -1)
    half = own.shape[split] // 2
    low = ring(lax.slice_in_dim(left, 0, half, axis=split), first, 1)
    high = ring(lax.slice_in_dim(right, half, 2 * half, axis=split), first, -1)
    across = jnp.concatenate([low, high], axis=split)
    bundle = jnp.stack([own, left, right, across])
    left, right = ring(bundle, second, 1), ring(bundle, second, -1)
    low, high = ring(left[:2], second, 1), ring(right[2:], second, -1)
    return bundle, left, right, low, high


def bundle_places():
    places = []
    for slot in range(4):
        for array in range(3):
            places.append((array, slot, slot, array))
        places.append((3 + slot // 2, slot % 2, slot, 3))
    return places


def place_pieces(refs, filled, sems, pos_ref, index_of):
    copies = []
    for half in range(2):
        first, second = (pos_ref[1], pos_ref[0]) if half == 0 else (pos_ref[0], pos_ref[1])
        for array, index, slot_first, slot_second in bundle_places():
            at_first = lax.rem(first + (SLOT_STEPS[slot_first] + 4), 4)
            at_second = lax.rem(second + (SLOT_STEPS[slot_second] + 4), 4)
            x, z = (at_second, at_first) if half == 0 else (at_first, at_second)
            copy = pltpu.make_async_copy(
                refs[half * 5 + array].at[index], filled.at[index_of(x, z, half)], sems.at[len(copies)]
            )
            copy.start()
            copies.append(copy)
    for copy in copies:
        copy.wait()


def product_kernel(transposed, pos_ref, tile_ref, *rest):
    pieces, (other_ref, mine_ref, filled, sems) = rest[:10], rest[10:]
    step = pl.program_id(0)

    if transposed:
        def index_of(x, z, half):
            return pl.ds(pl.multiple_of((z * 4 + x) * 32 + half * 16, 16), 16), slice(None)
    else:
        def index_of(x, z, half):
            return pl.ds(pl.multiple_of((x * 4 + z) * 192, 64), 192), pl.ds(half * 256, 256)

    @pl.when(step == 0)
    def _():
        place_pieces(pieces, filled, sems, pos_ref, index_of)

    dims = (((1,), (1,)), ((), ())) if transposed else (((1,), (0,)), ((), ()))
    product = lax.dot_general(tile_ref[0], filled[...], dims, preferred_element_type=F32).astype(BF16)

    @pl.when(step < 4)
    def _():
        other_ref[0] = product

    @pl.when(step >= 4)
    def _():
        mine_ref[0] = product


def panel_of(step, pos_ref):
    turn = lax.rem(step, 4)
    ahead = jnp.where(turn == 0, 2, jnp.where(turn == 1, 1, jnp.where(turn == 2, 3, 0)))
    core = jnp.where(step < 4, 1 - pos_ref[3], pos_ref[3])
    return lax.rem(pos_ref[2] + ahead, 4) * 2 + core


def product(kernel, pieces, pos, transposed):
    panels, rows, depth = kernel.shape
    width = 512
    out = jax.ShapeDtypeStruct((panels // 2, rows, width), BF16)
    return pl.pallas_call(
        lambda *refs: product_kernel(transposed, *refs),
        grid_spec=pltpu.PrefetchScalarGridSpec(
            num_scalar_prefetch=1,
            grid=(panels,),
            in_specs=[pl.BlockSpec((1, rows, depth), lambda i, p: (panel_of(i, p), 0, 0))] + [ANY] * 10,
            out_specs=[
                pl.BlockSpec((1, rows, width), lambda i, p: (jnp.minimum(i, 3), 0, 0)),
                pl.BlockSpec((1, rows, width), lambda i, p: (jnp.maximum(i - 4, 0), 0, 0)),
            ],
            scratch_shapes=[
                pltpu.VMEM((width, depth) if transposed else (depth, width), BF16),
                pltpu.SemaphoreType.DMA((32,)),
            ],
        ),
        out_shape=(out, out),
        compiler_params=pltpu.CompilerParams(vmem_limit_bytes=VMEM_LIMIT),
        cost_estimate=pl.CostEstimate(
            flops=2 * panels * rows * depth * width, bytes_accessed=16 << 20, transcendentals=0
        ),
    )(pos, kernel, *pieces)


def sum_over_col(other, mine):
    joined = mine.astype(F32) + cross(other).astype(F32)
    sent = joined[:3].astype(BF16)
    far, ahead, behind = ring(sent[0], "y", 2), ring(sent[1], "y", 1), ring(sent[2], "y", -1)
    return joined[3] + (far.astype(F32) + (ahead.astype(F32) + behind.astype(F32)))


def split_kernel(pos_ref, residual_ref, *out_refs):
    for step in range(4):
        column = pl.multiple_of(lax.rem(pos_ref[1] + step, 4) * 128, 128)
        out_refs[step][...] = residual_ref[:, pl.ds(column, 128)].astype(BF16)


def turn_kernel(pos_ref, *refs):
    pieces, out_refs, (tall, wide) = refs[:4], refs[4:8], refs[8:]
    for step in range(4):
        row = pl.multiple_of(lax.rem(pos_ref[1] + (4 - step), 4) * 192, 64)
        tall[pl.ds(row, 192), :] = pieces[step][...].astype(F32)
    wide[...] = tall[...].T
    for step in range(4):
        row = pl.multiple_of(lax.rem(pos_ref[0] + step, 4) * 32, 32)
        out_refs[step][...] = wide[pl.ds(row, 32), :].astype(BF16)


SMEM = pl.BlockSpec(memory_space=pltpu.SMEM)
VMEM = pl.BlockSpec(memory_space=pltpu.VMEM)


def whole_call(body, out_shape, scratch_shapes=(), scalars=1):
    def call(*args):
        return pl.pallas_call(
            body,
            in_specs=[SMEM] * scalars + [VMEM] * (len(args) - scalars),
            out_specs=jax.tree.map(lambda _: VMEM, out_shape),
            out_shape=out_shape,
            scratch_shapes=list(scratch_shapes),
            compiler_params=pltpu.CompilerParams(vmem_limit_bytes=VMEM_LIMIT),
        )(*args)

    return call


def to_columns(residual, pos):
    piece = jax.ShapeDtypeStruct((192, 128), BF16)
    pieces = whole_call(split_kernel, (piece,) * 4)(pos, residual)
    pieces = [pieces[0]] + [ring(pieces[step], "z", step) for step in (1, 2, 3)]
    piece = jax.ShapeDtypeStruct((32, 768), BF16)
    pieces = whole_call(
        turn_kernel, (piece,) * 4, (pltpu.VMEM((768, 128), F32), pltpu.VMEM((128, 768), F32))
    )(pos, *pieces)
    return [pieces[0]] + [ring(pieces[step], "x", step) for step in (1, 2, 3)]


def solve_kernel(last, pos_ref, lists_ref, counts_ref, *refs):
    pieces, inverse_ref, refs = refs[:4], refs[4], refs[5:]
    if last:
        before_ref, out_refs, (held, total) = refs[0], refs[1:5], refs[5:]
    else:
        low_ref, high_ref, full_ref, held, total = refs
    for step in range(4):
        at = pl.multiple_of(lax.rem(pos_ref[0] + (4 - step), 4) * 768, 128)
        held[:, pl.ds(at, 768)] = pieces[step][...]
    total[...] = jnp.zeros_like(total)

    def one(s, carry):
        starts = [pl.multiple_of(lists_ref[s, k] * BLOCK, BLOCK) for k in range(3)]
        picked = jnp.concatenate([held[:, pl.ds(start, BLOCK)] for start in starts], axis=1)
        fix = lax.dot_general(
            inverse_ref[s, :384, :], picked, (((1,), (1,)), ((), ())), preferred_element_type=F32
        )
        for k in range(3):
            total[pl.ds(starts[k], BLOCK), :] += fix[k * BLOCK:(k + 1) * BLOCK]
        return carry

    lax.fori_loop(0, 16, one, 0)
    panel = pos_ref[2] * 2 + pos_ref[3]
    for block in range(24):
        count = counts_ref[panel * 24 + block].astype(F32)
        at = slice(block * BLOCK, (block + 1) * BLOCK)
        mean = total[at, :].T / count
        if last:
            full = (mean + before_ref[:, at]).astype(BF16)
            out_refs[block // 6][:, (block % 6) * BLOCK:(block % 6 + 1) * BLOCK] = full
        else:
            full_ref[:, at] = mean
            low_ref[:, at] = mean[:16].astype(BF16)
            high_ref[:, at] = mean[16:].astype(BF16)


def solve(pieces, inverses, lists, counts, pos, before=None):
    last = before is not None
    if last:
        out_shape = (jax.ShapeDtypeStruct((32, 768), BF16),) * 4
    else:
        half = jax.ShapeDtypeStruct((16, 3072), BF16)
        out_shape = (half, half, jax.ShapeDtypeStruct((32, 3072), F32))
    args = [pos, lists, counts, *pieces, inverses] + ([before] if last else [])
    return whole_call(
        lambda *refs: solve_kernel(last, *refs),
        out_shape,
        (pltpu.VMEM((32, 3072), BF16), pltpu.VMEM((3072, 32), F32)),
        scalars=3,
    )(*args)


def turn_back_kernel(pos_ref, *refs):
    pieces, out_refs, (wide, tall) = refs[:4], refs[4:8], refs[8:]
    for step in range(4):
        row = pl.multiple_of(lax.rem(pos_ref[0] + (4 - step), 4) * 32, 32)
        wide[pl.ds(row, 32), :] = pieces[step][...].astype(F32)
    tall[...] = wide[...].T
    for step in range(4):
        row = pl.multiple_of(lax.rem(pos_ref[1] + step, 4) * 192, 64)
        out_refs[step][...] = tall[pl.ds(row, 192), :].astype(BF16)


def join_kernel(pos_ref, start_ref, *refs):
    pieces, out_ref = refs[:4], refs[4]
    for step in range(4):
        column = pl.multiple_of(lax.rem(pos_ref[1] + (4 - step), 4) * 128, 128)
        at = pl.ds(column, 128)
        out_ref[:, at] = start_ref[:, at] + pieces[step][...].astype(F32)


def from_columns(parts, start, pos):
    stacked = jnp.stack(parts)
    row = pos[0]
    own = [lax.dynamic_index_in_dim(stacked, lax.rem(row + step, 4), 0, keepdims=False) for step in range(4)]
    pieces = [own[0]] + [ring(own[step], "x", step) for step in (1, 2, 3)]
    piece = jax.ShapeDtypeStruct((192, 128), BF16)
    pieces = whole_call(
        turn_back_kernel, (piece,) * 4, (pltpu.VMEM((128, 768), F32), pltpu.VMEM((768, 128), F32))
    )(pos, *pieces)
    pieces = [pieces[0]] + [ring(pieces[step], "z", step) for step in (1, 2, 3)]
    return whole_call(join_kernel, jax.ShapeDtypeStruct((192, 512), F32))(pos, start, *pieces)


def body(kernel, right_side, initial, local_inverse, block_lists, counts):
    kernel, target, start = kernel[:, 0], right_side[0], initial[0]
    pos = jnp.stack([lax.axis_index(name) for name in ("x", "z", "y", "core")]).astype(jnp.int32)
    panel = pos[2] * 2 + pos[3]

    own_list = (block_lists - panel * 24).astype(BF16)
    list_rows = jnp.broadcast_to(jnp.pad(own_list, ((0, 0), (0, 381)))[:, None, :], (1, 16, 384))
    sent = jnp.concatenate([local_inverse.astype(BF16), list_rows], axis=1)
    inverses = lax.all_gather(sent, ("x", "z"), axis=0, tiled=True)
    lists = inverses[:, 384, :3].astype(jnp.int32)

    half = start.astype(BF16)
    pieces = [*gather_ring(half[:, :256], "z", "x", 0), *gather_ring(half[:, 256:], "x", "z", 0)]
    residual = target - sum_over_col(*product(kernel, pieces, pos, False))

    low, high, fix = solve(to_columns(residual, pos), inverses, lists, counts, pos)
    pieces = [*gather_ring(low, "z", "x", 1), *gather_ring(high, "x", "z", 1)]
    residual = residual - sum_over_col(*product(kernel, pieces, pos, True))

    parts = solve(to_columns(residual, pos), inverses, lists, counts, pos, fix)
    return (from_columns(parts, start, pos)[None], residual[None])


def solution(mesh):
    fine = Mesh(mesh.devices.reshape(4, 4, 4, 2), ("x", "z", "y", "core"))
    row, col = ("x", "z"), ("y", "core")
    return jax.shard_map(
        body,
        mesh=fine,
        in_specs=(
            P(None, row, None, col),
            P(col, row, None),
            P(col, row, None),
            P(row + col, None, None),
            P(row + col, None),
            P(),
        ),
        out_specs=(P(col, row, None), P(col, row, None)),
        check_vma=False,
    )
```

```python
import jax
import jax.numpy as jnp
from jax import lax
from jax.experimental import pallas as pl
from jax.experimental.pallas import tpu as pltpu
from jax.sharding import Mesh, PartitionSpec as P

BLOCK = 128
F32 = jnp.float32
BF16 = jnp.bfloat16
SMEM = pl.BlockSpec(memory_space=pltpu.SMEM)
VMEM = pl.BlockSpec(memory_space=pltpu.VMEM)
ANY = pl.BlockSpec(memory_space=pl.ANY)
VMEM_LIMIT = 24 * 1024 * 1024
QUARTER_STEPS = (
    (("z", 1), ("z", 3), ("x", 1), ("x", 3)),
    (("z", 3), ("z", 1), ("x", 3), ("x", 1)),
    (("x", 1), ("x", 3), ("z", 1), ("z", 3)),
    (("x", 3), ("x", 1), ("z", 3), ("z", 1)),
)


def swap(value, axis, mask):
    size = 2 if axis == "core" else 4
    return lax.ppermute(value, axis, [(i, i ^ mask) for i in range(size)])


def whole_call(body, out_shape, scratch_shapes=(), scalars=0, flops=1 << 20):
    def call(*args):
        return pl.pallas_call(
            body,
            in_specs=[SMEM] * scalars + [VMEM] * (len(args) - scalars),
            out_specs=jax.tree.map(lambda _: VMEM, out_shape),
            out_shape=out_shape,
            scratch_shapes=list(scratch_shapes),
            compiler_params=pltpu.CompilerParams(vmem_limit_bytes=VMEM_LIMIT),
            cost_estimate=pl.CostEstimate(flops=flops, bytes_accessed=1 << 20, transcendentals=0),
        )(*args)

    return call


def swap_turn(held, turn):
    return [swap(bundle, *QUARTER_STEPS[p][turn]) for p, bundle in enumerate(held)]


def joined(held, got):
    return [jnp.concatenate(pair) for pair in zip(held, got)]


def gather_swaps(parts, between=lambda turn, held: held):
    held = [part[None] for part in parts]
    for turn in range(3):
        held = between(turn, joined(held, swap_turn(held, turn)))
    return [bundle for pair in zip(held, swap_turn(held, 3)) for bundle in pair]


def source_masks(part, index):
    masks = {"x": 0, "z": 0}
    for turn, (axis, mask) in enumerate(QUARTER_STEPS[part]):
        if index >> turn & 1:
            masks[axis] ^= mask
    return masks["x"], masks["z"]


def hold_kernel(tile_ref, held_ref, sem):
    copy = pltpu.make_async_copy(tile_ref, held_ref, sem)
    copy.start()
    copy.wait()


def hold(tile):
    return pl.pallas_call(
        hold_kernel,
        in_specs=[ANY],
        out_specs=VMEM,
        out_shape=pltpu.VMEM(tile.shape, tile.dtype),
        scratch_shapes=[pltpu.SemaphoreType.DMA],
        compiler_params=pltpu.CompilerParams(vmem_limit_bytes=1024 * 1024),
    )(tile)


def fill_kernel(by_columns, pos_ref, bundles, filled):
    for part in range(4):
        for index in range(16):
            x_mask, z_mask = source_masks(part, index)
            x, z = pos_ref[0] ^ x_mask, pos_ref[1] ^ z_mask
            piece = bundles[part * 2 + index // 8]
            if by_columns:
                lanes = pl.ds(pl.multiple_of(x * 128, 128), 128)
                for half_block in range(12):
                    filled[(part * 12 + half_block) * 4 + z, :, lanes] = piece[index % 8, half_block]
            else:
                filled[pl.ds((x * 4 + z) * 12 + part * 3, 3)] = piece[index % 8]


def multiply(masks, pos_ref, tile_ref, filled, other_ref, mine_ref):
    def one(turn, carry):
        rows = tile_ref[pos_ref[2] ^ (masks[0] + turn)]
        vectors = filled[...].reshape(rows.shape[1], -1)
        result = jnp.dot(rows, vectors, preferred_element_type=F32).astype(BF16)
        for core in range(2):
            @pl.when(pos_ref[3] == core)
            def _():
                mine_ref[turn] = result[core * 192:(core + 1) * 192]
                other_ref[turn] = result[(1 - core) * 192:(2 - core) * 192]
        return carry

    lax.fori_loop(0, len(masks), one, 0)


def far_product_kernel(by_columns, pos_ref, tile_ref, *rest):
    bundles, (other_ref, mine_ref, filled) = rest[:8], rest[8:]
    fill_kernel(by_columns, pos_ref, bundles, filled)
    multiply((1, 2, 3), pos_ref, tile_ref, filled, other_ref, mine_ref)


def near_product_kernel(pos_ref, tile_ref, filled, other_ref, mine_ref):
    multiply((0,), pos_ref, tile_ref, filled, other_ref, mine_ref)


def product(tile, bundles, pos, by_columns):
    far = jax.ShapeDtypeStruct((3, 192, 512), BF16)
    near = jax.ShapeDtypeStruct((1, 192, 512), BF16)
    filled = jax.ShapeDtypeStruct((192, 16, 512), BF16)
    other, mine, filled = whole_call(
        lambda *refs: far_product_kernel(by_columns, *refs), (far, far, filled), scalars=1, flops=3 << 30
    )(pos, tile, *bundles)
    other_near, mine_near = whole_call(near_product_kernel, (near, near), scalars=1, flops=1 << 30)(pos, tile, filled)
    got = swap(other, "core", 1)
    sent = [(mine[at].astype(F32) + got[at].astype(F32)).astype(BF16) for at in range(3)]
    return sent, mine_near[0].astype(F32) + swap(other_near, "core", 1)[0].astype(F32)


def residual_kernel(pos_ref, before_ref, own_ref, *refs):
    sums, out_ref, column_refs = refs[:3], refs[3], refs[4:]
    total = own_ref[...] + (sums[0][...].astype(F32) + (sums[1][...].astype(F32) + sums[2][...].astype(F32)))
    out_ref[...] = before_ref[...] - total
    for mask in range(4):
        lanes = pl.ds(pl.multiple_of((pos_ref[0] ^ mask) * 128, 128), 128)
        column_refs[mask][...] = out_ref[:, lanes].astype(BF16)


def sums_over_y(sent):
    return [swap(sent[mask - 1], "y", mask) for mask in (1, 2, 3)]


def residual_of(before, near, sums, pos):
    piece = jax.ShapeDtypeStruct((192, 128), BF16)
    out_shape = (jax.ShapeDtypeStruct((192, 512), F32),) + (piece,) * 4
    return whole_call(residual_kernel, out_shape, scalars=1)(pos, before, near, *sums)


def exchange(pieces):
    bundle = jnp.stack([pieces[0]] + [swap(pieces[mask], "x", mask) for mask in (1, 2, 3)])
    return [bundle] + [swap(bundle, "z", mask) for mask in (1, 2, 3)]


def inverse_kernel(pos_ref, lists_ref, inverse_ref, *out_refs):
    panel = pos_ref[2] * 2 + pos_ref[3]
    lane = lax.broadcasted_iota(jnp.int32, (16, 384), 1)
    ids = [lists_ref[0, k] - panel * 24 for k in range(3)]
    row = jnp.where(lane == 0, ids[0], jnp.where(lane == 1, ids[1], ids[2])).astype(F32).astype(BF16)
    for mask in range(4):
        for half_block in range(6):
            at = pl.multiple_of(half_block * 64 + (pos_ref[1] ^ mask) * 16, 16)
            out_refs[mask][half_block * 16:(half_block + 1) * 16, :] = inverse_ref[pl.ds(at, 16), :].astype(BF16)
        out_refs[mask][96:, :] = row


def solve_kernel(last, pos_ref, lists_ref, counts_ref, *refs):
    bundles, inverse_refs, refs = refs[:4], refs[4:6], refs[6:]
    if last:
        before_ref, sent_ref, held, total = refs
    else:
        full_ref, *quarter_refs, held, total = refs
    for z_mask in range(4):
        for x_mask in range(4):
            group = (pos_ref[0] ^ x_mask) * 4 + (pos_ref[1] ^ z_mask)
            held[pl.ds(pl.multiple_of(group * 192, 64), 192), :] = bundles[z_mask][x_mask]
    total[...] = jnp.zeros_like(total)
    for s in range(16):
        ids = [lists_ref[s, k] for k in range(3)]
        picked = jnp.concatenate([held[pl.ds(pl.multiple_of(q * BLOCK, BLOCK), BLOCK), :] for q in ids])
        fix = jnp.dot(inverse_refs[s // 8][s % 8, :96, :], picked, preferred_element_type=F32)
        for k in range(3):
            total[ids[k]] += fix[k * 32:(k + 1) * 32]
    panel = pos_ref[2] * 2 + pos_ref[3]
    for block in range(24):
        mean = total[block] / counts_ref[panel * 24 + block].astype(F32)
        if last:
            mean = (mean + before_ref[block]).astype(BF16)
            for half in range(2):
                at = block * 2 + half
                sent_ref[at // 3, at % 3 * 16:(at % 3 + 1) * 16, :] = mean[half * 16:(half + 1) * 16]
        else:
            full_ref[block] = mean
            for half in range(2):
                quarter_refs[block // 6][block % 6 * 2 + half] = mean[half * 16:(half + 1) * 16].astype(BF16)


def solve(bundles, inverses, lists, counts, pos, before=None):
    last = before is not None
    if last:
        out_shape = jax.ShapeDtypeStruct((16, 48, 128), BF16)
    else:
        out_shape = (jax.ShapeDtypeStruct((24, 32, 128), F32),) + (jax.ShapeDtypeStruct((12, 16, 128), BF16),) * 4
    scratch = [pltpu.VMEM((3072, 128), BF16), pltpu.VMEM((24, 32, 128), F32)]
    args = [pos, lists, counts, *bundles, *inverses] + ([before] if last else [])
    return whole_call(lambda *refs: solve_kernel(last, *refs), out_shape, scratch, scalars=3)(*args)


def join_kernel(start_ref, pieces_ref, out_ref):
    for x in range(4):
        for z in range(4):
            for third in range(3):
                at = slice(third * 64 + z * 16, third * 64 + z * 16 + 16), slice(x * 128, (x + 1) * 128)
                piece = pieces_ref[x * 4 + z, third * 16:(third + 1) * 16, :]
                out_ref[at] = start_ref[at] + piece.astype(F32)


def body(kernel, right_side, initial, local_inverse, block_lists, counts):
    target, start = right_side[0], initial[0]
    pos = jnp.stack([lax.axis_index(name) for name in ("x", "z", "y", "core")]).astype(jnp.int32)
    rows = kernel.reshape(4, 384, 3072)

    piece = jax.ShapeDtypeStruct((112, 384), BF16)
    sent = whole_call(inverse_kernel, (piece,) * 4, scalars=2)(pos, block_lists, local_inverse[0])
    inverse = [sent]

    def between(turn, held):
        if turn == 0:
            inverse.append(swap(jnp.stack(sent[1:3]), "z", 1))
        elif turn == 1:
            inverse.append(swap(jnp.stack([sent[3], inverse[1][1]]), "z", 3))
        else:
            inverse.append(jnp.stack([sent[0], inverse[1][0], inverse[2][0], inverse[2][1]]))
            inverse.append(swap(inverse[3], "x", 1))
        held, inverse[-1] = lax.optimization_barrier((held, inverse[-1]))
        return held

    half = start.astype(BF16).reshape(4, 3, 16, 512)
    bundles = gather_swaps([half[at] for at in range(4)], between)
    tile, bundles = lax.optimization_barrier((hold(rows), bundles))
    far, near = product(tile, bundles, pos, False)
    inverses = jnp.concatenate(inverse[3:])
    inverses = inverses, swap(inverses, "x", 3)
    sums, inverses = lax.optimization_barrier((sums_over_y(far), inverses))
    lists = jnp.concatenate([bundle[:, 96, :3] for bundle in inverses]).astype(jnp.int32)

    residual, *pieces = residual_of(target, near, sums, pos)
    fix, *quarters = solve(exchange(pieces), inverses, lists, counts, pos)
    held = []

    def between(turn, parts):
        if turn == 2:
            tied = lax.optimization_barrier((parts, rows))
            held.append(tied[1])
            return tied[0]
        return parts

    bundles = gather_swaps(quarters, between)
    tile, bundles = lax.optimization_barrier((hold(held[0]), bundles))
    far, near = product(tile, bundles, pos, True)
    residual, *pieces = residual_of(residual, near, sums_over_y(far), pos)
    sent = solve(exchange(pieces), inverses, lists, counts, pos, fix)
    pieces = lax.all_to_all(sent, ("x", "z"), 0, 0, tiled=True)
    result = whole_call(join_kernel, jax.ShapeDtypeStruct((192, 512), F32))(start, pieces)
    return (result[None], residual[None])


def solution(mesh):
    fine = Mesh(mesh.devices.reshape(4, 4, 4, 2), ("x", "z", "y", "core"))
    row, col = ("x", "z"), ("y", "core")
    return jax.shard_map(
        body,
        mesh=fine,
        in_specs=(
            P(None, row, None, col),
            P(col, row, None),
            P(col, row, None),
            P(row + col, None, None),
            P(row + col, None),
            P(),
        ),
        out_specs=(P(col, row, None), P(col, row, None)),
        check_vma=False,
    )
```

```python
import jax
import jax.numpy as jnp
from jax import lax
from jax.experimental import pallas as pl
from jax.experimental.pallas import tpu as pltpu
from jax.sharding import Mesh, PartitionSpec as P

BLOCK = 128
F32 = jnp.float32
BF16 = jnp.bfloat16
SMEM = pl.BlockSpec(memory_space=pltpu.SMEM)
VMEM = pl.BlockSpec(memory_space=pltpu.VMEM)
ANY = pl.BlockSpec(memory_space=pl.ANY)
VMEM_LIMIT = 24 * 1024 * 1024
QUARTER_STEPS = (
    (("z", 1), ("z", 3), ("x", 1), ("x", 3)),
    (("z", 3), ("z", 1), ("x", 3), ("x", 1)),
    (("x", 1), ("x", 3), ("z", 1), ("z", 3)),
    (("x", 3), ("x", 1), ("z", 3), ("z", 1)),
)


def swap(value, axis, mask):
    size = 2 if axis == "core" else 4
    return lax.ppermute(value, axis, [(i, i ^ mask) for i in range(size)])


def whole_call(body, out_shape, scratch_shapes=(), scalars=0, flops=1 << 20):
    def call(*args):
        return pl.pallas_call(
            body,
            in_specs=[SMEM] * scalars + [VMEM] * (len(args) - scalars),
            out_specs=jax.tree.map(lambda _: VMEM, out_shape),
            out_shape=out_shape,
            scratch_shapes=list(scratch_shapes),
            compiler_params=pltpu.CompilerParams(vmem_limit_bytes=VMEM_LIMIT),
            cost_estimate=pl.CostEstimate(flops=flops, bytes_accessed=1 << 20, transcendentals=0),
        )(*args)

    return call


def swap_turn(held, turn):
    return [swap(bundle, *QUARTER_STEPS[p][turn]) for p, bundle in enumerate(held)]


def joined(held, got):
    return [jnp.concatenate(pair) for pair in zip(held, got)]


def gather_swaps(parts, between=lambda turn, held: held):
    held = [part[None] for part in parts]
    for turn in range(3):
        held = between(turn, joined(held, swap_turn(held, turn)))
    return [bundle for pair in zip(held, swap_turn(held, 3)) for bundle in pair]


def source_masks(part, index):
    masks = {"x": 0, "z": 0}
    for turn, (axis, mask) in enumerate(QUARTER_STEPS[part]):
        if index >> turn & 1:
            masks[axis] ^= mask
    return masks["x"], masks["z"]


def after(done, value):
    return lax.optimization_barrier((done, value))[1]


def hold_kernel(tile_ref, held_ref, sem):
    copy = pltpu.make_async_copy(tile_ref, held_ref, sem)
    copy.start()
    copy.wait()


def hold(tile):
    return pl.pallas_call(
        hold_kernel,
        in_specs=[ANY],
        out_specs=VMEM,
        out_shape=pltpu.VMEM(tile.shape, tile.dtype),
        scratch_shapes=[pltpu.SemaphoreType.DMA],
        compiler_params=pltpu.CompilerParams(vmem_limit_bytes=1024 * 1024),
    )(tile)


def fill_kernel(by_columns, pos_ref, bundles, filled):
    for part in range(4):
        for index in range(16):
            x_mask, z_mask = source_masks(part, index)
            x, z = pos_ref[0] ^ x_mask, pos_ref[1] ^ z_mask
            piece = bundles[part * 2 + index // 8]
            if by_columns:
                lanes = pl.ds(pl.multiple_of(x * 128, 128), 128)
                for half_block in range(12):
                    filled[(part * 12 + half_block) * 4 + z, :, lanes] = piece[index % 8, half_block]
            else:
                filled[pl.ds((x * 4 + z) * 12 + part * 3, 3)] = piece[index % 8]


def multiply(masks, pos_ref, tile_ref, filled, other_ref, mine_ref):
    def one(turn, carry):
        rows = tile_ref[pos_ref[2] ^ (masks[0] + turn)]
        vectors = filled[...].reshape(rows.shape[1], -1)
        result = jnp.dot(rows, vectors, preferred_element_type=F32).astype(BF16)
        for core in range(2):
            @pl.when(pos_ref[3] == core)
            def _():
                mine_ref[turn] = result[core * 192:(core + 1) * 192]
                other_ref[turn] = result[(1 - core) * 192:(2 - core) * 192]
        return carry

    lax.fori_loop(0, len(masks), one, 0)


def far_product_kernel(by_columns, pos_ref, tile_ref, *rest):
    bundles, (other_ref, mine_ref, filled) = rest[:8], rest[8:]
    fill_kernel(by_columns, pos_ref, bundles, filled)
    multiply((1, 2, 3), pos_ref, tile_ref, filled, other_ref, mine_ref)


def near_product_kernel(pos_ref, tile_ref, filled, other_ref, mine_ref):
    multiply((0,), pos_ref, tile_ref, filled, other_ref, mine_ref)


def product(tile, bundles, pos, by_columns):
    far = jax.ShapeDtypeStruct((3, 192, 512), BF16)
    near = jax.ShapeDtypeStruct((1, 192, 512), BF16)
    filled = jax.ShapeDtypeStruct((192, 16, 512), BF16)
    other, mine, filled = whole_call(
        lambda *refs: far_product_kernel(by_columns, *refs), (far, far, filled), scalars=1, flops=3 << 30
    )(pos, tile, *bundles)
    other_near, mine_near = whole_call(near_product_kernel, (near, near), scalars=1, flops=1 << 30)(pos, tile, filled)
    got = swap(other, "core", 1)
    sent = [(mine[at].astype(F32) + got[at].astype(F32)).astype(BF16) for at in range(3)]
    return sent, mine_near[0].astype(F32) + swap(other_near, "core", 1)[0].astype(F32)


def residual_kernel(before_ref, own_ref, *refs):
    sums, (out_ref, sent_ref) = refs[:3], refs[3:]
    total = own_ref[...] + (sums[0][...].astype(F32) + (sums[1][...].astype(F32) + sums[2][...].astype(F32)))
    left = before_ref[...] - total
    out_ref[...] = left
    half = left.astype(BF16)
    for x in range(4):
        for z in range(4):
            sent_ref[x * 4 + z] = half[:, x * 128:(x + 1) * 128]


def sums_over_y(sent):
    return [swap(sent[mask - 1], "y", mask) for mask in (1, 2, 3)]


def residual_of(before, near, sums):
    out_shape = (jax.ShapeDtypeStruct((192, 512), F32), jax.ShapeDtypeStruct((16, 192, 128), BF16))
    return whole_call(residual_kernel, out_shape)(before, near, *sums)


def exchange(sent):
    return lax.all_to_all(sent, ("x", "z"), 0, 0, tiled=True).reshape(3072, 128)


def inverse_kernel(pos_ref, lists_ref, inverse_ref, *out_refs):
    panel = pos_ref[2] * 2 + pos_ref[3]
    lane = lax.broadcasted_iota(jnp.int32, (16, 384), 1)
    ids = [lists_ref[0, k] - panel * 24 for k in range(3)]
    row = jnp.where(lane == 0, ids[0], jnp.where(lane == 1, ids[1], ids[2])).astype(F32).astype(BF16)
    for mask in range(4):
        for half_block in range(6):
            at = pl.multiple_of(half_block * 64 + (pos_ref[1] ^ mask) * 16, 16)
            out_refs[mask][half_block * 16:(half_block + 1) * 16, :] = inverse_ref[pl.ds(at, 16), :].astype(BF16)
        out_refs[mask][96:, :] = row


def solve_kernel(last, pos_ref, lists_ref, counts_ref, *refs):
    held, *inverse_refs = refs[:5]
    refs = refs[5:]
    if last:
        before_ref, sent_ref, total = refs
    else:
        full_ref, *quarter_refs, total = refs
    total[...] = jnp.zeros_like(total)
    for s in range(16):
        ids = [lists_ref[s, k] for k in range(3)]
        picked = jnp.concatenate([held[pl.ds(pl.multiple_of(q * BLOCK, BLOCK), BLOCK), :] for q in ids])
        fix = jnp.dot(inverse_refs[s // 4][s % 4, :96, :], picked, preferred_element_type=F32)
        for k in range(3):
            total[ids[k]] += fix[k * 32:(k + 1) * 32]
    panel = pos_ref[2] * 2 + pos_ref[3]
    for block in range(24):
        mean = total[block] / counts_ref[panel * 24 + block].astype(F32)
        if last:
            mean = (mean + before_ref[block]).astype(BF16)
            for half in range(2):
                at = block * 2 + half
                sent_ref[at // 3, at % 3 * 16:(at % 3 + 1) * 16, :] = mean[half * 16:(half + 1) * 16]
        else:
            full_ref[block] = mean
            for half in range(2):
                quarter_refs[block // 6][block % 6 * 2 + half] = mean[half * 16:(half + 1) * 16].astype(BF16)


def solve(held, inverses, lists, counts, pos, before=None):
    last = before is not None
    if last:
        out_shape = jax.ShapeDtypeStruct((16, 48, 128), BF16)
    else:
        out_shape = (jax.ShapeDtypeStruct((24, 32, 128), F32),) + (jax.ShapeDtypeStruct((12, 16, 128), BF16),) * 4
    scratch = [pltpu.VMEM((24, 32, 128), F32)]
    args = [pos, lists, counts, held, *inverses] + ([before] if last else [])
    return whole_call(lambda *refs: solve_kernel(last, *refs), out_shape, scratch, scalars=3)(*args)


def join_kernel(start_ref, pieces_ref, out_ref):
    for x in range(4):
        for z in range(4):
            for third in range(3):
                at = slice(third * 64 + z * 16, third * 64 + z * 16 + 16), slice(x * 128, (x + 1) * 128)
                piece = pieces_ref[x * 4 + z, third * 16:(third + 1) * 16, :]
                out_ref[at] = start_ref[at] + piece.astype(F32)


def body(kernel, right_side, initial, local_inverse, block_lists, counts):
    target, start = right_side[0], initial[0]
    pos = jnp.stack([lax.axis_index(name) for name in ("x", "z", "y", "core")]).astype(jnp.int32)
    rows = kernel.reshape(4, 384, 3072)

    piece = jax.ShapeDtypeStruct((112, 384), BF16)
    sent = whole_call(inverse_kernel, (piece,) * 4, scalars=2)(pos, block_lists, local_inverse[0])
    near = {}

    def between(turn, held):
        if turn == 0:
            near["sent"] = after(held, sent)
            near["first"] = swap(jnp.stack(near["sent"][1:3]), "z", 1)
        elif turn == 1:
            start, first = after(held, (near["sent"], near["first"]))
            near["second"] = swap(jnp.stack([start[3], first[1]]), "z", 3)
            near["low"] = jnp.stack([start[0], first[0]])
            near["low_far"] = swap(near["low"], "x", 1)
        else:
            near["high"] = after(held, near["second"])
            near["high_far"] = swap(near["high"], "x", 3)
        return held

    half = start.astype(BF16).reshape(4, 3, 16, 512)
    bundles = gather_swaps([half[at] for at in range(4)], between)
    tile, bundles, low, high = lax.optimization_barrier(
        (hold(rows), bundles, [near["low"], near["low_far"]], [near["high"], near["high_far"]])
    )
    far, near = product(tile, bundles, pos, False)
    low, high = jnp.concatenate(low), jnp.concatenate(high)
    inverses = low, swap(low, "x", 3), high, swap(high, "x", 1)
    sums, inverses = lax.optimization_barrier((sums_over_y(far), inverses))
    lists = jnp.concatenate([bundle[:, 96, :3] for bundle in inverses]).astype(jnp.int32)

    residual, sent = residual_of(target, near, sums)
    fix, *quarters = solve(exchange(sent), inverses, lists, counts, pos)
    held = []

    def between(turn, parts):
        if turn == 2:
            tied = lax.optimization_barrier((parts, rows))
            held.append(tied[1])
            return tied[0]
        return parts

    bundles = gather_swaps(quarters, between)
    tile, bundles = lax.optimization_barrier((hold(held[0]), bundles))
    far, near = product(tile, bundles, pos, True)
    residual, sent = residual_of(residual, near, sums_over_y(far))
    sent = solve(exchange(sent), inverses, lists, counts, pos, fix)
    pieces = lax.all_to_all(sent, ("x", "z"), 0, 0, tiled=True)
    result = whole_call(join_kernel, jax.ShapeDtypeStruct((192, 512), F32))(start, pieces)
    return (result[None], residual[None])


def solution(mesh):
    fine = Mesh(mesh.devices.reshape(4, 4, 4, 2), ("x", "z", "y", "core"))
    row, col = ("x", "z"), ("y", "core")
    return jax.shard_map(
        body,
        mesh=fine,
        in_specs=(
            P(None, row, None, col),
            P(col, row, None),
            P(col, row, None),
            P(row + col, None, None),
            P(row + col, None),
            P(),
        ),
        out_specs=(P(col, row, None), P(col, row, None)),
        check_vma=False,
    )
```

```python
import jax
import jax.numpy as jnp
from jax import lax
from jax.experimental import pallas as pl
from jax.experimental.pallas import tpu as pltpu
from jax.sharding import Mesh, PartitionSpec as P

BLOCK = 128
F32 = jnp.float32
BF16 = jnp.bfloat16
SMEM = pl.BlockSpec(memory_space=pltpu.SMEM)
VMEM = pl.BlockSpec(memory_space=pltpu.VMEM)
ANY = pl.BlockSpec(memory_space=pl.ANY)
VMEM_LIMIT = 24 * 1024 * 1024
QUARTER_STEPS = (
    (("z", 1), ("z", 3), ("x", 1), ("x", 3)),
    (("z", 3), ("z", 1), ("x", 3), ("x", 1)),
    (("x", 1), ("x", 3), ("z", 1), ("z", 3)),
    (("x", 3), ("x", 1), ("z", 3), ("z", 1)),
)


def swap(value, axis, mask):
    size = 2 if axis == "core" else 4
    return lax.ppermute(value, axis, [(i, i ^ mask) for i in range(size)])


def whole_call(body, out_shape, scratch_shapes=(), scalars=0, flops=1 << 20):
    def call(*args):
        return pl.pallas_call(
            body,
            in_specs=[SMEM] * scalars + [VMEM] * (len(args) - scalars),
            out_specs=jax.tree.map(lambda _: VMEM, out_shape),
            out_shape=out_shape,
            scratch_shapes=list(scratch_shapes),
            compiler_params=pltpu.CompilerParams(vmem_limit_bytes=VMEM_LIMIT),
            cost_estimate=pl.CostEstimate(flops=flops, bytes_accessed=1 << 20, transcendentals=0),
        )(*args)

    return call


def swap_turn(held, turn):
    return [swap(bundle, *QUARTER_STEPS[p][turn]) for p, bundle in enumerate(held)]


def joined(held, got):
    return [jnp.concatenate(pair) for pair in zip(held, got)]


def gather_swaps(parts, between=lambda turn, held: held):
    held = [part[None] for part in parts]
    for turn in range(3):
        held = between(turn, joined(held, swap_turn(held, turn)))
    return [bundle for pair in zip(held, swap_turn(held, 3)) for bundle in pair]


def source_masks(part, index):
    masks = {"x": 0, "z": 0}
    for turn, (axis, mask) in enumerate(QUARTER_STEPS[part]):
        if index >> turn & 1:
            masks[axis] ^= mask
    return masks["x"], masks["z"]


def after(done, value):
    return lax.optimization_barrier((done, value))[1]


def hold_kernel(tile_ref, held_ref, sem):
    copy = pltpu.make_async_copy(tile_ref, held_ref, sem)
    copy.start()
    copy.wait()


def hold(tile):
    return pl.pallas_call(
        hold_kernel,
        in_specs=[ANY],
        out_specs=VMEM,
        out_shape=pltpu.VMEM(tile.shape, tile.dtype),
        scratch_shapes=[pltpu.SemaphoreType.DMA],
        compiler_params=pltpu.CompilerParams(vmem_limit_bytes=1024 * 1024),
    )(tile)


def fill_kernel(by_columns, pos_ref, bundles, filled):
    for part in range(4):
        for index in range(16):
            x_mask, z_mask = source_masks(part, index)
            x, z = pos_ref[0] ^ x_mask, pos_ref[1] ^ z_mask
            piece = bundles[part * 2 + index // 8]
            if by_columns:
                lanes = pl.ds(pl.multiple_of(x * 128, 128), 128)
                for half_block in range(12):
                    filled[(part * 12 + half_block) * 4 + z, :, lanes] = piece[index % 8, half_block]
            else:
                filled[pl.ds((x * 4 + z) * 12 + part * 3, 3)] = piece[index % 8]


def multiply(masks, pos_ref, tile_ref, filled, other_ref, mine_ref):
    vectors = filled[...].reshape(tile_ref.shape[2], -1)
    for turn, mask in enumerate(masks):
        rows = tile_ref[pos_ref[2] ^ mask]
        result = jnp.dot(rows, vectors, preferred_element_type=F32).astype(BF16)
        for core in range(2):
            @pl.when(pos_ref[3] == core)
            def _():
                mine_ref[turn] = result[core * 192:(core + 1) * 192]
                other_ref[turn] = result[(1 - core) * 192:(2 - core) * 192]


def first_product_kernel(by_columns, masks, pos_ref, tile_ref, *rest):
    bundles, (other_ref, mine_ref, filled) = rest[:8], rest[8:]
    fill_kernel(by_columns, pos_ref, bundles, filled)
    multiply(masks, pos_ref, tile_ref, filled, other_ref, mine_ref)


def sums_over_col(tile, bundles, pos, by_columns):
    def out(masks):
        return (jax.ShapeDtypeStruct((len(masks), 192, 512), BF16),) * 2

    def later(masks, filled):
        return whole_call(
            lambda *refs: multiply(masks, *refs), out(masks), scalars=1, flops=len(masks) << 30
        )(pos, tile, filled)

    def send(both, masks):
        other, mine = both
        got = swap(other, "core", 1)
        both = [mine[turn].astype(F32) + got[turn].astype(F32) for turn in range(len(masks))]
        return both if masks == (0,) else [value.astype(BF16) for value in both]

    filled = jax.ShapeDtypeStruct((192, 16, 512), BF16)
    *across, filled = whole_call(
        lambda *refs: first_product_kernel(by_columns, (2,), *refs), (*out((2,)), filled), scalars=1, flops=1 << 30
    )(pos, tile, *bundles)
    beside = later((1, 3), filled)
    across = send(across, (2,))
    near = later((0,), after(across, filled))
    beside, near = send(beside, (1, 3)), send(near, (0,))
    return [swap(beside[0], "y", 1), swap(across[0], "y", 2), swap(beside[1], "y", 3)], near[0]


def residual_kernel(before_ref, own_ref, *refs):
    sums, (out_ref, sent_ref) = refs[:3], refs[3:]
    total = own_ref[...] + (sums[0][...].astype(F32) + (sums[1][...].astype(F32) + sums[2][...].astype(F32)))
    left = before_ref[...] - total
    out_ref[...] = left
    half = left.astype(BF16)
    for x in range(4):
        for z in range(4):
            sent_ref[x * 4 + z] = half[:, x * 128:(x + 1) * 128]


def residual_of(before, near, sums):
    out_shape = (jax.ShapeDtypeStruct((192, 512), F32), jax.ShapeDtypeStruct((16, 192, 128), BF16))
    return whole_call(residual_kernel, out_shape)(before, near, *sums)


def exchange(sent):
    return lax.all_to_all(sent, ("x", "z"), 0, 0, tiled=True).reshape(3072, 128)


def inverse_kernel(pos_ref, lists_ref, inverse_ref, *out_refs):
    panel = pos_ref[2] * 2 + pos_ref[3]
    lane = lax.broadcasted_iota(jnp.int32, (16, 384), 1)
    ids = [lists_ref[0, k] - panel * 24 for k in range(3)]
    row = jnp.where(lane == 0, ids[0], jnp.where(lane == 1, ids[1], ids[2])).astype(F32).astype(BF16)
    for mask in range(4):
        for half_block in range(6):
            at = pl.multiple_of(half_block * 64 + (pos_ref[1] ^ mask) * 16, 16)
            out_refs[mask][half_block * 16:(half_block + 1) * 16, :] = inverse_ref[pl.ds(at, 16), :].astype(BF16)
        out_refs[mask][96:, :] = row


def solve_kernel(last, pos_ref, lists_ref, counts_ref, *refs):
    held, *inverse_refs = refs[:5]
    refs = refs[5:]
    if last:
        before_ref, sent_ref, total = refs
    else:
        full_ref, *quarter_refs, total = refs
    total[...] = jnp.zeros_like(total)
    for s in range(16):
        ids = [lists_ref[s, k] for k in range(3)]
        picked = jnp.concatenate([held[pl.ds(pl.multiple_of(q * BLOCK, BLOCK), BLOCK), :] for q in ids])
        fix = jnp.dot(inverse_refs[s // 4][s % 4, :96, :], picked, preferred_element_type=F32)
        for k in range(3):
            total[ids[k]] += fix[k * 32:(k + 1) * 32]
    panel = pos_ref[2] * 2 + pos_ref[3]
    for block in range(24):
        mean = total[block] / counts_ref[panel * 24 + block].astype(F32)
        if last:
            mean = (mean + before_ref[block]).astype(BF16)
            for half in range(2):
                at = block * 2 + half
                sent_ref[at // 3, at % 3 * 16:(at % 3 + 1) * 16, :] = mean[half * 16:(half + 1) * 16]
        else:
            full_ref[block] = mean
            for half in range(2):
                quarter_refs[block // 6][block % 6 * 2 + half] = mean[half * 16:(half + 1) * 16].astype(BF16)


def solve(held, inverses, lists, counts, pos, before=None):
    last = before is not None
    if last:
        out_shape = jax.ShapeDtypeStruct((16, 48, 128), BF16)
    else:
        out_shape = (jax.ShapeDtypeStruct((24, 32, 128), F32),) + (jax.ShapeDtypeStruct((12, 16, 128), BF16),) * 4
    scratch = [pltpu.VMEM((24, 32, 128), F32)]
    args = [pos, lists, counts, held, *inverses] + ([before] if last else [])
    return whole_call(lambda *refs: solve_kernel(last, *refs), out_shape, scratch, scalars=3)(*args)


def join_kernel(start_ref, pieces_ref, out_ref):
    for x in range(4):
        for z in range(4):
            for third in range(3):
                at = slice(third * 64 + z * 16, third * 64 + z * 16 + 16), slice(x * 128, (x + 1) * 128)
                piece = pieces_ref[x * 4 + z, third * 16:(third + 1) * 16, :]
                out_ref[at] = start_ref[at] + piece.astype(F32)


def body(kernel, right_side, initial, local_inverse, block_lists, counts):
    target, start = right_side[0], initial[0]
    pos = jnp.stack([lax.axis_index(name) for name in ("x", "z", "y", "core")]).astype(jnp.int32)
    rows = kernel.reshape(4, 384, 3072)

    piece = jax.ShapeDtypeStruct((112, 384), BF16)
    sent = whole_call(inverse_kernel, (piece,) * 4, scalars=2)(pos, block_lists, local_inverse[0])
    near = {}

    def between(turn, held):
        if turn == 0:
            near["sent"] = after(held, sent)
            near["first"] = swap(jnp.stack(near["sent"][1:3]), "z", 1)
        elif turn == 1:
            start, first = after(held, (near["sent"], near["first"]))
            near["second"] = swap(jnp.stack([start[3], first[1]]), "z", 3)
            near["low"] = jnp.stack([start[0], first[0]])
            near["low_far"] = swap(near["low"], "x", 1)
        else:
            near["tile"] = hold(rows)
            near["high"] = after((held, near["tile"]), near["second"])
            near["high_far"] = swap(near["high"], "x", 3)
        return held

    half = start.astype(BF16).reshape(4, 3, 16, 512)
    bundles = gather_swaps([half[at] for at in range(4)], between)
    tile, bundles, low, high = lax.optimization_barrier(
        (near["tile"], bundles, [near["low"], near["low_far"]], [near["high"], near["high_far"]])
    )
    low, high = jnp.concatenate(low), jnp.concatenate(high)
    inverses = low, swap(low, "x", 3), high, swap(high, "x", 1)
    sums, near = sums_over_col(tile, bundles, pos, False)
    sums, inverses = lax.optimization_barrier((sums, inverses))
    lists = jnp.concatenate([bundle[:, 96, :3] for bundle in inverses]).astype(jnp.int32)

    residual, sent = residual_of(target, near, sums)
    fix, *quarters = solve(exchange(sent), inverses, lists, counts, pos)
    held = []

    def between(turn, parts):
        if turn == 2:
            tied = lax.optimization_barrier((parts, rows))
            held.append(tied[1])
            return tied[0]
        return parts

    bundles = gather_swaps(quarters, between)
    tile, bundles = lax.optimization_barrier((hold(held[0]), bundles))
    sums, near = sums_over_col(tile, bundles, pos, True)
    residual, sent = residual_of(residual, near, sums)
    sent = solve(exchange(sent), inverses, lists, counts, pos, fix)
    pieces = lax.all_to_all(sent, ("x", "z"), 0, 0, tiled=True)
    result = whole_call(join_kernel, jax.ShapeDtypeStruct((192, 512), F32))(start, pieces)
    return (result[None], residual[None])


def solution(mesh):
    fine = Mesh(mesh.devices.reshape(4, 4, 4, 2), ("x", "z", "y", "core"))
    row, col = ("x", "z"), ("y", "core")
    return jax.shard_map(
        body,
        mesh=fine,
        in_specs=(
            P(None, row, None, col),
            P(col, row, None),
            P(col, row, None),
            P(row + col, None, None),
            P(row + col, None),
            P(),
        ),
        out_specs=(P(col, row, None), P(col, row, None)),
        check_vma=False,
    )
```

```python
import jax
import jax.numpy as jnp
from jax import lax
from jax.experimental import pallas as pl
from jax.experimental.pallas import tpu as pltpu
from jax.sharding import Mesh, PartitionSpec as P

BLOCK = 128
F32 = jnp.float32
BF16 = jnp.bfloat16
SMEM = pl.BlockSpec(memory_space=pltpu.SMEM)
VMEM = pl.BlockSpec(memory_space=pltpu.VMEM)
ANY = pl.BlockSpec(memory_space=pl.ANY)
VMEM_LIMIT = 24 * 1024 * 1024
QUARTER_STEPS = (
    (("z", 1), ("z", 3), ("x", 1), ("x", 3)),
    (("z", 1), ("z", 3), ("x", 3), ("x", 1)),
    (("x", 1), ("x", 3), ("z", 1), ("z", 3)),
    (("x", 1), ("x", 3), ("z", 3), ("z", 1)),
)


def swap(value, axis, mask):
    size = 2 if axis == "core" else 4
    return lax.ppermute(value, axis, [(i, i ^ mask) for i in range(size)])


def whole_call(body, out_shape, scratch_shapes=(), scalars=0, flops=1 << 20):
    def call(*args):
        return pl.pallas_call(
            body,
            in_specs=[SMEM] * scalars + [VMEM] * (len(args) - scalars),
            out_specs=jax.tree.map(lambda _: VMEM, out_shape),
            out_shape=out_shape,
            scratch_shapes=list(scratch_shapes),
            compiler_params=pltpu.CompilerParams(vmem_limit_bytes=VMEM_LIMIT),
            cost_estimate=pl.CostEstimate(flops=flops, bytes_accessed=1 << 20, transcendentals=0),
        )(*args)

    return call


def swap_turn(held, turn):
    return [swap(bundle, *QUARTER_STEPS[p][turn]) for p, bundle in enumerate(held)]


def joined(held, got):
    return [jnp.concatenate(pair) for pair in zip(held, got)]


def gather_swaps(parts, between=lambda turn, held: held):
    held = [jnp.stack(parts[at:at + 2])[None] for at in (0, 2)]
    for turn in range(2):
        got = [swap(pair, *QUARTER_STEPS[2 * p][turn]) for p, pair in enumerate(held)]
        held = between(turn, joined(held, got))
    held = [pair[:, at] for pair in held for at in range(2)]
    held = between(2, joined(held, swap_turn(held, 2)))
    return [bundle for pair in zip(held, swap_turn(held, 3)) for bundle in pair]


def source_masks(part, index):
    masks = {"x": 0, "z": 0}
    for turn, (axis, mask) in enumerate(QUARTER_STEPS[part]):
        if index >> turn & 1:
            masks[axis] ^= mask
    return masks["x"], masks["z"]


def after(done, value):
    return lax.optimization_barrier((done, value))[1]


def hold_kernel(tile_ref, held_ref, sem):
    copy = pltpu.make_async_copy(tile_ref, held_ref, sem)
    copy.start()
    copy.wait()


def hold(tile):
    return pl.pallas_call(
        hold_kernel,
        in_specs=[ANY],
        out_specs=VMEM,
        out_shape=pltpu.VMEM(tile.shape, tile.dtype),
        scratch_shapes=[pltpu.SemaphoreType.DMA],
        compiler_params=pltpu.CompilerParams(vmem_limit_bytes=1024 * 1024),
    )(tile)


def fill_kernel(by_columns, pos_ref, bundles, filled):
    for part in range(4):
        for index in range(16):
            x_mask, z_mask = source_masks(part, index)
            x, z = pos_ref[0] ^ x_mask, pos_ref[1] ^ z_mask
            piece = bundles[part * 2 + index // 8]
            if by_columns:
                lanes = pl.ds(pl.multiple_of(x * 128, 128), 128)
                for half_block in range(12):
                    filled[(part * 12 + half_block) * 4 + z, :, lanes] = piece[index % 8, half_block]
            else:
                filled[pl.ds((x * 4 + z) * 12 + part * 3, 3)] = piece[index % 8]


def multiply(masks, pos_ref, tile_ref, filled, other_ref, mine_ref):
    vectors = filled[...].reshape(tile_ref.shape[2], -1)
    for turn, mask in enumerate(masks):
        rows = tile_ref[pos_ref[2] ^ mask]
        result = jnp.dot(rows, vectors, preferred_element_type=F32).astype(BF16)
        for core in range(2):
            @pl.when(pos_ref[3] == core)
            def _():
                mine_ref[turn] = result[core * 192:(core + 1) * 192]
                other_ref[turn] = result[(1 - core) * 192:(2 - core) * 192]


def first_product_kernel(by_columns, masks, pos_ref, tile_ref, *rest):
    bundles, (other_ref, mine_ref, filled) = rest[:8], rest[8:]
    fill_kernel(by_columns, pos_ref, bundles, filled)
    multiply(masks, pos_ref, tile_ref, filled, other_ref, mine_ref)


def sums_over_col(tile, bundles, pos, by_columns):
    def out(masks):
        return (jax.ShapeDtypeStruct((len(masks), 192, 512), BF16),) * 2

    def later(masks, filled):
        return whole_call(
            lambda *refs: multiply(masks, *refs), out(masks), scalars=1, flops=len(masks) << 30
        )(pos, tile, filled)

    def send(both, masks):
        other, mine = both
        got = swap(other, "core", 1)
        both = [mine[turn].astype(F32) + got[turn].astype(F32) for turn in range(len(masks))]
        return both if masks == (0,) else [value.astype(BF16) for value in both]

    filled = jax.ShapeDtypeStruct((192, 16, 512), BF16)
    *across, filled = whole_call(
        lambda *refs: first_product_kernel(by_columns, (2,), *refs), (*out((2,)), filled), scalars=1, flops=1 << 30
    )(pos, tile, *bundles)
    beside = later((1, 3), filled)
    across = send(across, (2,))
    near = later((0,), after(across, filled))
    beside, near = send(beside, (1, 3)), send(near, (0,))
    return [swap(beside[0], "y", 1), swap(across[0], "y", 2), swap(beside[1], "y", 3)], near[0]


def residual_kernel(before_ref, own_ref, *refs):
    sums, (out_ref, sent_ref) = refs[:3], refs[3:]
    total = own_ref[...] + (sums[0][...].astype(F32) + (sums[1][...].astype(F32) + sums[2][...].astype(F32)))
    left = before_ref[...] - total
    out_ref[...] = left
    half = left.astype(BF16)
    for x in range(4):
        for z in range(4):
            sent_ref[x * 4 + z] = half[:, x * 128:(x + 1) * 128]


def residual_of(before, near, sums):
    out_shape = (jax.ShapeDtypeStruct((192, 512), F32), jax.ShapeDtypeStruct((16, 192, 128), BF16))
    return whole_call(residual_kernel, out_shape)(before, near, *sums)


def exchange(sent):
    return lax.all_to_all(sent, ("x", "z"), 0, 0, tiled=True).reshape(3072, 128)


def inverse_kernel(pos_ref, lists_ref, inverse_ref, *out_refs):
    panel = pos_ref[2] * 2 + pos_ref[3]
    lane = lax.broadcasted_iota(jnp.int32, (16, 384), 1)
    ids = [lists_ref[0, k] - panel * 24 for k in range(3)]
    row = jnp.where(lane == 0, ids[0], jnp.where(lane == 1, ids[1], ids[2])).astype(F32).astype(BF16)
    for mask in range(4):
        for half_block in range(6):
            at = pl.multiple_of(half_block * 64 + (pos_ref[1] ^ mask) * 16, 16)
            out_refs[mask][half_block * 16:(half_block + 1) * 16, :] = inverse_ref[pl.ds(at, 16), :].astype(BF16)
        out_refs[mask][96:, :] = row


def solve_kernel(last, pos_ref, lists_ref, counts_ref, *refs):
    held, *inverse_refs = refs[:5]
    refs = refs[5:]
    if last:
        before_ref, sent_ref, total = refs
    else:
        full_ref, *quarter_refs, total = refs
    total[...] = jnp.zeros_like(total)
    for s in range(16):
        ids = [lists_ref[s, k] for k in range(3)]
        picked = jnp.concatenate([held[pl.ds(pl.multiple_of(q * BLOCK, BLOCK), BLOCK), :] for q in ids])
        fix = jnp.dot(inverse_refs[s // 4][s % 4, :96, :], picked, preferred_element_type=F32)
        for k in range(3):
            total[ids[k]] += fix[k * 32:(k + 1) * 32]
    panel = pos_ref[2] * 2 + pos_ref[3]
    for block in range(24):
        mean = total[block] / counts_ref[panel * 24 + block].astype(F32)
        if last:
            mean = (mean + before_ref[block]).astype(BF16)
            for half in range(2):
                at = block * 2 + half
                sent_ref[at // 3, at % 3 * 16:(at % 3 + 1) * 16, :] = mean[half * 16:(half + 1) * 16]
        else:
            full_ref[block] = mean
            for half in range(2):
                quarter_refs[block // 6][block % 6 * 2 + half] = mean[half * 16:(half + 1) * 16].astype(BF16)


def solve(held, inverses, lists, counts, pos, before=None):
    last = before is not None
    if last:
        out_shape = jax.ShapeDtypeStruct((16, 48, 128), BF16)
    else:
        out_shape = (jax.ShapeDtypeStruct((24, 32, 128), F32),) + (jax.ShapeDtypeStruct((12, 16, 128), BF16),) * 4
    scratch = [pltpu.VMEM((24, 32, 128), F32)]
    args = [pos, lists, counts, held, *inverses] + ([before] if last else [])
    return whole_call(lambda *refs: solve_kernel(last, *refs), out_shape, scratch, scalars=3)(*args)


def join_kernel(start_ref, pieces_ref, out_ref):
    for x in range(4):
        for z in range(4):
            for third in range(3):
                at = slice(third * 64 + z * 16, third * 64 + z * 16 + 16), slice(x * 128, (x + 1) * 128)
                piece = pieces_ref[x * 4 + z, third * 16:(third + 1) * 16, :]
                out_ref[at] = start_ref[at] + piece.astype(F32)


def body(kernel, right_side, initial, local_inverse, block_lists, counts):
    target, start = right_side[0], initial[0]
    pos = jnp.stack([lax.axis_index(name) for name in ("x", "z", "y", "core")]).astype(jnp.int32)
    rows = kernel.reshape(4, 384, 3072)

    piece = jax.ShapeDtypeStruct((112, 384), BF16)
    sent = whole_call(inverse_kernel, (piece,) * 4, scalars=2)(pos, block_lists, local_inverse[0])
    near = {}

    def between(turn, held):
        if turn == 0:
            near["sent"] = after(held, sent)
            near["first"] = swap(jnp.stack(near["sent"][1:3]), "z", 1)
        elif turn == 1:
            start, first = after(held, (near["sent"], near["first"]))
            near["second"] = swap(jnp.stack([start[3], first[1]]), "z", 3)
            near["low"] = jnp.stack([start[0], first[0]])
            near["low_far"] = swap(near["low"], "x", 1)
        else:
            near["tile"] = hold(rows)
            near["high"] = after((held, near["tile"]), near["second"])
            near["high_far"] = swap(near["high"], "x", 3)
        return held

    half = start.astype(BF16).reshape(4, 3, 16, 512)
    bundles = gather_swaps([half[at] for at in range(4)], between)
    tile, bundles, low, high = lax.optimization_barrier(
        (near["tile"], bundles, [near["low"], near["low_far"]], [near["high"], near["high_far"]])
    )
    low, high = jnp.concatenate(low), jnp.concatenate(high)
    inverses = low, swap(low, "x", 3), high, swap(high, "x", 1)
    sums, near = sums_over_col(tile, bundles, pos, False)
    sums, inverses = lax.optimization_barrier((sums, inverses))
    lists = jnp.concatenate([bundle[:, 96, :3] for bundle in inverses]).astype(jnp.int32)

    residual, sent = residual_of(target, near, sums)
    fix, *quarters = solve(exchange(sent), inverses, lists, counts, pos)
    held = []

    def between(turn, parts):
        if turn == 2:
            tied = lax.optimization_barrier((parts, rows))
            held.append(tied[1])
            return tied[0]
        return parts

    bundles = gather_swaps(quarters, between)
    tile, bundles = lax.optimization_barrier((hold(held[0]), bundles))
    sums, near = sums_over_col(tile, bundles, pos, True)
    residual, sent = residual_of(residual, near, sums)
    sent = solve(exchange(sent), inverses, lists, counts, pos, fix)
    pieces = lax.all_to_all(sent, ("x", "z"), 0, 0, tiled=True)
    result = whole_call(join_kernel, jax.ShapeDtypeStruct((192, 512), F32))(start, pieces)
    return (result[None], residual[None])


def solution(mesh):
    fine = Mesh(mesh.devices.reshape(4, 4, 4, 2), ("x", "z", "y", "core"))
    row, col = ("x", "z"), ("y", "core")
    return jax.shard_map(
        body,
        mesh=fine,
        in_specs=(
            P(None, row, None, col),
            P(col, row, None),
            P(col, row, None),
            P(row + col, None, None),
            P(row + col, None),
            P(),
        ),
        out_specs=(P(col, row, None), P(col, row, None)),
        check_vma=False,
    )
```
